512 devices in a mesh: gx: 8 (over y_hi, x), gy: 16 (over z), gz: 4 (over y_lo, core).
Axes of the slice: x: 4, y: 4 (y_hi: 2, y_lo: 2; y = y_hi * 2 + y_lo), z: 16, core: 2. Of those that a mesh axis runs over, the one named last changes fastest.
Arguments:
- rhs_fine: float32 [16, 32, 8, 2048], P('gx', 'gy', 'gz'), may hold values from -6 to 6
- fine_blocks: float32 [16, 32, 8, 7, 4096], P('gx', 'gy', 'gz'), may hold values from -2.5 to 2.5
- fine_links: int32 [16, 32, 8, 6], P('gx', 'gy', 'gz'), may hold values 0 or 1
- fine_smoother: float32 [16, 32, 8, 4096], P('gx', 'gy', 'gz'), may hold values from -2 to 2
- fine_prolong: float32 [16, 32, 8, 4096], P('gx', 'gy', 'gz'), may hold values from -0.75 to 0.75
- mid_blocks: float32 [8, 16, 4, 7, 4096], P('gx', 'gy'), may hold values from -2.5 to 2.5
- mid_links: int32 [8, 16, 4, 6], P('gx', 'gy'), may hold values 0 or 1
- mid_smoother: float32 [8, 16, 4, 4096], P('gx', 'gy'), may hold values from -2 to 2
- mid_prolong: float32 [8, 16, 4, 4096], P('gx', 'gy'), may hold values from -0.75 to 0.75
- coarse_blocks: float32 [8, 8, 2, 7, 4096], P('gx'), may hold values from -2.5 to 2.5
- coarse_links: int32 [8, 8, 2, 6], P('gx'), may hold values 0 or 1
- coarse_smoother: float32 [8, 8, 2, 4096], P('gx'), may hold values from -2 to 2
- lower_bounds: float32 [3], replicated, may hold values from 0.08 to 0.3
- upper_bounds: float32 [3], replicated, may hold values from 1.6 to 2.6
Outputs:
- solution: float32 [16, 32, 8, 2048], P('gx', 'gy', 'gz')
- residual: float32 [16, 32, 8, 2048], P('gx', 'gy', 'gz')
The draws below stay inside these ranges and needn't reach their ends.
All inputs are finite; a program needn't handle non-finite values. No bound on the sum of `fine_links` or of `mid_links` or of `coarse_links` on one device may be relied on, other than what follows from the above.
Results may differ from the reference program's by a relative error of at most 0.0003.
Values sent between devices are 32-bit elements; how exact they have to be, the bound alone decides.
A program may use at most 128 MiB of HBM per device.

```python
import math
import jax
import jax.numpy as jnp
from jax import lax

BLOCK = 64
RHS = 32
SWEEPS = 2
COARSE_SWEEPS = 4
NX = 16
NY = 32
NZ = 8
MX = 8
MY = 16
MZ = 4
LY = 8
LZ = 2


def noise_field(key, shape):
    return jnp.clip(jax.random.normal(key, shape, jnp.float32), -6.0, 6.0)


def draw_operator(key, nodes):
    first, second = jax.random.split(jax.random.fold_in(key, 11))
    noise = noise_field(first, nodes + (7, BLOCK, BLOCK)) / math.sqrt(BLOCK)
    scales = jnp.exp(jax.random.uniform(second, nodes + (7, 1, 1), jnp.float32, math.log(0.6), math.log(1.6)))
    identity = jnp.eye(BLOCK, dtype=jnp.float32)
    link = jnp.arange(7).reshape(7, 1, 1)
    centre = identity + 0.35 * noise
    side = -(0.12 * identity + 0.1 * noise)
    blocks = scales * jnp.where(link == 0, centre, side)
    return blocks.reshape(nodes + (7, BLOCK * BLOCK))


def draw_inverse(key, nodes):
    first, second = jax.random.split(jax.random.fold_in(key, 23))
    noise = noise_field(first, nodes + (BLOCK, BLOCK)) / math.sqrt(BLOCK)
    scales = jnp.exp(jax.random.uniform(second, nodes + (1, 1), jnp.float32, math.log(0.5), math.log(1.2)))
    identity = jnp.eye(BLOCK, dtype=jnp.float32)
    return (scales * (identity - 0.3 * noise)).reshape(nodes + (BLOCK * BLOCK,))


def draw_rhs_fine(key, part):
    shape = (NX, NY, NZ, BLOCK * RHS)
    return jnp.clip(jax.random.normal(key, shape, jnp.float32), -6.0, 6.0)


def draw_fine_blocks(key, part):
    return draw_operator(key, (NX, NY, NZ))


def draw_mid_blocks(key, part):
    return draw_operator(key, (MX, MY, MZ))


def draw_coarse_blocks(key, part):
    return draw_operator(key, (MX, LY, LZ))


def draw_fine_smoother(key, part):
    return draw_inverse(key, (NX, NY, NZ))


def draw_mid_smoother(key, part):
    return draw_inverse(key, (MX, MY, MZ))


def draw_coarse_smoother(key, part):
    return draw_inverse(key, (MX, LY, LZ))


def plant(result, key, smallest, top_value):
    longest = result.shape.index(max(result.shape))
    spots = []
    for shift in (0, 1):
        where = [jax.random.randint(jax.random.fold_in(key, axis), (), 0, length) for axis, length in enumerate(result.shape)]
        where[longest] = (where[longest] + shift) % result.shape[longest]
        spots.append(tuple(where))
    return result.at[spots[0]].set(smallest).at[spots[1]].set(top_value)


def level_of(key, shape, cuts, least, top_value):
    def one(axis_at, parts):
        draws = jax.random.uniform(jax.random.fold_in(jax.random.fold_in(key, 6), axis_at), (parts,), jnp.float32, least / len(cuts), top_value / len(cuts))
        return jnp.repeat(jnp.exp(draws), shape[axis_at] // parts).reshape((-1,) + (1,) * (len(shape) - axis_at - 1))

    gain = one(*cuts[0])
    for cut in cuts[1:]:
        gain = gain * one(*cut)
    return gain


def scatter_about(own_key, dims, scale, limit, shards=(), held_as=jnp.bfloat16):
    drawn = scale * jax.random.normal(own_key, dims, jnp.float32)
    if shards:
        drawn = drawn * level_of(own_key, dims, shards, -0.22, 0.18)
    return jnp.clip(drawn, -limit, limit).astype(held_as)


def setup_inputs(seed: int = 0) -> dict:
    splits = jax.random.split(jax.random.key(seed), 15)
    return {
        "rhs_fine": draw_rhs_fine(jax.random.fold_in(splits[14], 71), 0),
        "fine_blocks": draw_fine_blocks(jax.random.fold_in(splits[14], 71), 0),
        "fine_links": plant((jax.random.randint(splits[2], (NX, NY, NZ, 6), 0, 4) < 3).astype(jnp.int32), jax.random.fold_in(splits[2], 1), 0, 1),
        "fine_smoother": draw_fine_smoother(jax.random.fold_in(splits[14], 71), 0),
        "fine_prolong": scatter_about(splits[4], (NX, NY, NZ, BLOCK * BLOCK), BLOCK ** -0.5, 0.75, ((0, 8), (1, 16), (2, 4)), jnp.float32),
        "mid_blocks": draw_mid_blocks(jax.random.fold_in(splits[14], 71), 0),
        "mid_links": plant((jax.random.randint(splits[6], (MX, MY, MZ, 6), 0, 4) < 3).astype(jnp.int32), jax.random.fold_in(splits[6], 1), 0, 1),
        "mid_smoother": draw_mid_smoother(jax.random.fold_in(splits[14], 71), 0),
        "mid_prolong": scatter_about(splits[8], (MX, MY, MZ, BLOCK * BLOCK), BLOCK ** -0.5, 0.75, ((0, 8), (1, 16)), jnp.float32),
        "coarse_blocks": draw_coarse_blocks(jax.random.fold_in(splits[14], 71), 0),
        "coarse_links": plant((jax.random.randint(splits[10], (MX, LY, LZ, 6), 0, 4) < 3).astype(jnp.int32), jax.random.fold_in(splits[10], 1), 0, 1),
        "coarse_smoother": draw_coarse_smoother(jax.random.fold_in(splits[14], 71), 0),
        "lower_bounds": jnp.clip(jnp.exp(jax.random.uniform(splits[12], (3,), jnp.float32, math.log(0.08), math.log(0.3))), 0.08, 0.3),
        "upper_bounds": jnp.clip(jax.random.uniform(splits[13], (3,), jnp.float32, 1.6, 2.6), 1.6, 2.6),
    }


HIGH = lax.Precision.HIGHEST


def apply_level(padded, blocks, links):
    sizes = blocks.shape[:3]
    count = sizes[0] * sizes[1] * sizes[2]
    centre = padded[1:-1, 1:-1, 1:-1]
    beside = [padded[:-2, 1:-1, 1:-1], padded[2:, 1:-1, 1:-1],
              padded[1:-1, :-2, 1:-1], padded[1:-1, 2:, 1:-1],
              padded[1:-1, 1:-1, :-2], padded[1:-1, 1:-1, 2:]]
    mats = blocks.reshape((count, 7, BLOCK, BLOCK))
    flags = links.reshape((count, 6)).astype(jnp.float32)
    out = jnp.matmul(mats[:, 0], centre.reshape((count, BLOCK, RHS)), precision=HIGH)
    for link in range(6):
        term = jnp.matmul(mats[:, link + 1], beside[link].reshape((count, BLOCK, RHS)), precision=HIGH)
        out = out + flags[:, link, None, None] * term
    return out.reshape(sizes + (BLOCK * RHS,))


def smooth_with(inverse, field):
    sizes = field.shape[:3]
    out = jnp.einsum('abcij,abcjr->abcir', inverse.reshape(sizes + (BLOCK, BLOCK)),
                     field.reshape(sizes + (BLOCK, RHS)), precision=HIGH)
    return out.reshape(sizes + (BLOCK * RHS,))


def transpose_with(prolong, field):
    sizes = field.shape[:3]
    out = jnp.einsum('abcji,abcjr->abcir', prolong.reshape(sizes + (BLOCK, BLOCK)),
                     field.reshape(sizes + (BLOCK, RHS)), precision=HIGH)
    return out.reshape(sizes + (BLOCK * RHS,))


def pair_sum(terms, step_x, step_y, step_z):
    size_x, size_y, size_z, width = terms.shape
    grouped = terms.reshape(size_x // step_x, step_x, size_y // step_y, step_y, size_z // step_z, step_z, width)
    return jnp.sum(grouped, axis=(1, 3, 5))


def upsample(field, step_x, step_y, step_z):
    return jnp.repeat(jnp.repeat(jnp.repeat(field, step_x, 0), step_y, 1), step_z, 2)


def chebyshev(operate, inverse, rhs, start, sweeps, lower, upper):
    theta = (upper + lower) * 0.5
    delta = (upper - lower) * 0.5
    sigma = theta / delta
    rho = 1.0 / sigma
    if start is None:
        resid = rhs
    else:
        resid = rhs - operate(start)
    direction = smooth_with(inverse, resid) / theta
    field = direction if start is None else start + direction
    for sweep in range(sweeps - 1):
        resid = resid - operate(direction)
        rho_next = 1.0 / (2.0 * sigma - rho)
        direction = rho_next * rho * direction + (2.0 * rho_next / delta) * smooth_with(inverse, resid)
        rho = rho_next
        field = field + direction
    return field


def pad_three(field):
    return jnp.pad(field, ((1, 1), (1, 1), (1, 1), (0, 0)))


def reference(rhs_fine, fine_blocks, fine_links, fine_smoother, fine_prolong, mid_blocks, mid_links, mid_smoother, mid_prolong, coarse_blocks, coarse_links, coarse_smoother, lower_bounds, upper_bounds):
    def fine_op(field):
        return apply_level(pad_three(field), fine_blocks, fine_links)

    def mid_op(field):
        return apply_level(pad_three(field), mid_blocks, mid_links)

    def coarse_op(field):
        return apply_level(pad_three(field), coarse_blocks, coarse_links)

    fine_first = chebyshev(fine_op, fine_smoother, rhs_fine, None, SWEEPS, lower_bounds[0], upper_bounds[0])
    mid_rhs = pair_sum(transpose_with(fine_prolong, rhs_fine - fine_op(fine_first)), 2, 2, 2)
    mid_first = chebyshev(mid_op, mid_smoother, mid_rhs, None, SWEEPS, lower_bounds[1], upper_bounds[1])
    coarse_rhs = pair_sum(transpose_with(mid_prolong, mid_rhs - mid_op(mid_first)), 1, 2, 2)
    coarse_fix = chebyshev(coarse_op, coarse_smoother, coarse_rhs, None, COARSE_SWEEPS, lower_bounds[2], upper_bounds[2])
    mid_start = mid_first + smooth_with(mid_prolong, upsample(coarse_fix, 1, 2, 2))
    mid_fix = chebyshev(mid_op, mid_smoother, mid_rhs, mid_start, SWEEPS, lower_bounds[1], upper_bounds[1])
    fine_start = fine_first + smooth_with(fine_prolong, upsample(mid_fix, 2, 2, 2))
    solution = chebyshev(fine_op, fine_smoother, rhs_fine, fine_start, SWEEPS, lower_bounds[0], upper_bounds[0])
    residual = rhs_fine - fine_op(solution)
    return (solution, residual)
```

```python
import jax
import jax.numpy as jnp
from jax import lax
from jax.experimental import pallas as pl
from jax.experimental.pallas import tpu as pltpu
from jax.sharding import PartitionSpec as P

F32 = jnp.float32
BF16 = jnp.bfloat16
MESH = pl.DeviceIdType.MESH


def lane(shape=(64, 128)):
    return lax.broadcasted_iota(jnp.int32, shape, 1)


def low(shape=(64, 128)):
    return lane(shape) < 64


def pick(group, parts):
    return jnp.where(
        group < 2,
        jnp.where(group == 0, parts[0], parts[1]),
        jnp.where(group == 2, parts[2], parts[3]),
    )


def roll(x, shift):
    return pltpu.roll(x, shift, 1) if shift else x


def split(v):
    high = v.astype(BF16)
    return high, (v - high.astype(F32)).astype(BF16)


def wide(v):
    return jnp.concatenate(split(v), axis=1)


def tall(v):
    high, rest = split(v)
    return jnp.concatenate([high, rest, high, rest], axis=0)


def matmul(left, right):
    return jnp.dot(left, right, preferred_element_type=F32)


def rows_of(ref, node, many):
    return ref[pl.ds(node, 32, stride=many), :]


def weave(ref, left, right):
    first = low((32, 128))
    left_turned, right_turned = roll(left, 64), roll(right, 64)
    ref[pl.ds(0, 32, stride=2), :] = jnp.where(first, left, right_turned)
    ref[pl.ds(1, 32, stride=2), :] = jnp.where(first, left_turned, right)
    return ref[...]


def double(block):
    high, rest = split(block)
    return jnp.concatenate([high, rest], axis=1)


def fold_fine(product, group):
    total = (product[:256, :128] + product[:256, 128:]) + (
        product[256:, :128] + product[256:, 128:]
    )
    return pick(group, [total[64 * g : 64 * g + 64] for g in range(4)])


def kernel(
    rhs_hbm,
    fblocks_hbm,
    flinks,
    fsmooth_hbm,
    fprolong_hbm,
    mblocks_hbm,
    mlinks,
    msmooth_hbm,
    mprolong_hbm,
    cblocks_hbm,
    clinks,
    csmooth_hbm,
    lowers,
    uppers,
    solution_ref,
    residual_ref,
    rhs_raw,
    fblocks,
    fsmooth,
    fprolong,
    mblocks,
    msmooth,
    mprolong,
    cblocks,
    csmooth,
    in_sems,
    packed,
    woven,
    inner_l,
    outer_l,
    smooth_l,
    prolong_l,
    restrict_l,
    one_outer,
    one_centre,
    one_smooth,
    one_prolong,
    face_send,
    face_pack,
    face_recv,
    node_send,
    node_recv,
    sib_send,
    sib_recv,
    face_out_sem,
    face_in_sem,
    node_out_sem,
    node_in_sem,
    sib_out_sem,
    sib_in_sem,
):
    size = {name: lax.axis_size(name) for name in ("gx", "gy", "gz")}
    at = {name: lax.axis_index(name) for name in ("gx", "gy", "gz")}

    def beside(name, step):
        return {name: lax.rem(at[name] + (step + size[name]), size[name])}

    mate_y = at["gy"] + 1 - 2 * lax.rem(at["gy"], 2)
    mate_z = at["gz"] + 1 - 2 * lax.rem(at["gz"], 2)
    near = [
        beside("gx", -1),
        beside("gx", 1),
        beside("gy", -1),
        beside("gy", 1),
        beside("gz", -1),
        beside("gz", 1),
    ]
    coarse_near = [
        beside("gx", -1),
        beside("gx", 1),
        beside("gy", -2),
        beside("gy", 2),
        beside("gz", 2),
    ]
    siblings = [{"gy": mate_y}, {"gz": mate_z}, {"gy": mate_y, "gz": mate_z}]
    parent_y = lax.div(at["gy"], 2)
    parent_z = lax.div(at["gz"], 2)

    loads = [
        pltpu.make_async_copy(src, dst, in_sems.at[i])
        for i, (src, dst) in enumerate(
            [
                (rhs_hbm, rhs_raw),
                (fsmooth_hbm, fsmooth),
                (fblocks_hbm, fblocks),
                (fprolong_hbm, fprolong),
                (mblocks_hbm, mblocks),
                (msmooth_hbm, msmooth),
                (mprolong_hbm, mprolong),
                (cblocks_hbm.at[parent_y], cblocks),
                (csmooth_hbm.at[parent_y], csmooth),
            ]
        )
    ]
    for load in loads:
        load.start()

    barrier = pltpu.get_barrier_semaphore()
    greeted = near + coarse_near[2:] + siblings[2:]
    for device in greeted:
        pl.semaphore_signal(barrier, inc=1, device_id=device, device_id_type=MESH)

    def has(name, step):
        if step < 0:
            return jnp.where(at[name] >= -step, 1.0, 0.0).astype(F32)
        return jnp.where(at[name] < size[name] - step, 1.0, 0.0).astype(F32)

    reach = [has("gx", -1), has("gx", 1), has("gy", -1), has("gy", 1), has("gz", -1), has("gz", 1)]
    coarse_reach = [has("gx", -1), has("gx", 1), has("gy", -2), has("gy", 2), has("gz", -2), has("gz", 2)]

    group = lax.shift_right_logical(lane(), 5)
    group16 = lax.shift_right_logical(lane((16, 128)), 5)
    first_half = low()
    even = lax.rem(group, 2) == 0

    def coefficients(level):
        upper = jnp.full((1, 128), uppers[level], F32)
        lower = jnp.full((1, 128), lowers[level], F32)
        theta = (upper + lower) * 0.5
        delta = (upper - lower) * 0.5
        sigma = theta / delta
        rho = 1.0 / sigma
        steps = []
        for _ in range(3 if level == 2 else 1):
            later = 1.0 / (2.0 * sigma - rho)
            steps.append((later * rho, 2.0 * later / delta))
            rho = later
        return 1.0 / theta, steps

    def from_natural(raw, out):
        for a in range(2):
            nodes = [raw[a, g // 2, pl.ds(g % 2, 16, stride=2), :] for g in range(4)]
            for q in range(4):
                out[a, pl.ds(q, 16, stride=4), :] = pick(
                    group16, [roll(nodes[g], 32 * ((g - q) % 4)) for g in range(4)]
                )

    def to_natural(field, out):
        for a in range(2):
            packed[a] = field[a]
        for a in range(2):
            rows = [packed[a, pl.ds(q, 16, stride=4), :] for q in range(4)]
            for g in range(4):
                out[a, g // 2, pl.ds(g % 2, 16, stride=2), :] = pick(
                    group16, [roll(rows[q], 32 * ((q - g) % 4)) for q in range(4)]
                )

    def each(times, body):
        def step(n, carry):
            body(n)
            return carry

        lax.fori_loop(0, times, step, 0)

    def put(ref, a, g, column, value, rest_at=256):
        high, rest = split(value)
        rows = pl.ds(pl.multiple_of(g * 64, 64), 64)
        rest_rows = pl.ds(pl.multiple_of(rest_at + g * 64, 64), 64)
        ref[a, rows, column : column + 128] = high
        ref[a, rest_rows, column : column + 128] = rest

    def double_fine(raw, out, slot, turned=None):
        for a in range(2):
            for b in range(2):
                both = []
                for c in range(2):
                    g = 2 * b + c
                    block = rows_of(raw.at[a, b], c, 2)
                    block = weave(woven.at[slot + 4 * a + g], block, block)
                    out[a, 64 * g : 64 * g + 64, :] = double(block)
                    both.append(block)
                if turned is not None:
                    column = 128 * (2 * a + b)
                    high, rest = split(jnp.transpose(jnp.concatenate(both, axis=0))[0:64, :])
                    turned[0:64, column : column + 128] = high
                    turned[64:128, column : column + 128] = rest

    def prepare_fine():
        def body(n):
            a, b = lax.div(n, 2), lax.rem(n, 2)

            def far(axis, here):
                return jnp.where(here == 0, reach[2 * axis], reach[2 * axis + 1])

            for c in range(2):
                g = 2 * b + c

                def block(d, far=None):
                    flag = flinks[a, b, c, d - 1].astype(F32)
                    if far is not None:
                        flag = flag * far
                    return rows_of(fblocks.at[a, b, d], c, 2) * flag

                slots = woven.at[pl.ds(n * 8 + c * 4, 4)]
                centre = rows_of(fblocks.at[a, b, 0], c, 2)
                put(inner_l, a, g, 0, weave(slots.at[0], centre, block(2 - a)))
                put(inner_l, a, g, 128, weave(slots.at[1], block(4 - b), block(6 - c)))
                put(outer_l, a, g, 0, weave(slots.at[2], block(1 + a, far(0, a)), block(3 + b, far(1, b))))
                last = block(5 + c, far(2, c))
                put(outer_l, a, g, 128, weave(slots.at[3], last, jnp.zeros_like(last)))

        each(4, body)

    def one_block(raw, row, many, out, slot):
        block = rows_of(raw, row, many)
        block = weave(woven.at[slot], block, block)
        out[...] = double(block)
        return block

    def one_turned(block, out):
        out[...] = double(jnp.transpose(jnp.concatenate([block, block], axis=0))[0:64, :])

    def one_operator(raw, row, many, flag, level, slot):
        one_block(raw.at[0], row, many, one_centre.at[level], slot)
        for pair in range(3):
            d = 2 * pair + 1
            put(
                one_outer,
                level,
                0,
                128 * pair,
                weave(
                    woven.at[slot + 1 + pair],
                    rows_of(raw.at[d], row, many) * flag(d),
                    rows_of(raw.at[d + 1], row, many) * flag(d + 1),
                ),
                64,
            )

    def faces(slot):
        copies = []
        for side in range(6):
            if side == 0:
                src, dst = face_send.at[slot, 0], 1
            elif side == 1:
                src, dst = face_send.at[slot, 1], 0
            else:
                src, dst = face_pack.at[slot, side - 2], side ^ 1
            copies.append(
                pltpu.make_async_remote_copy(
                    src_ref=src,
                    dst_ref=face_recv.at[slot, dst],
                    send_sem=face_out_sem.at[slot, side],
                    recv_sem=face_in_sem.at[slot, dst],
                    device_id=near[side],
                    device_id_type=MESH,
                )
            )
        return copies

    def send_faces(slot, field):
        copies = faces(slot)
        zero, one = field
        face_send[slot, 0] = zero
        face_send[slot, 1] = one
        copies[0].start()
        copies[1].start()
        face_pack[slot, 0] = jnp.where(first_half, zero, roll(one, 64))
        copies[2].start()
        face_pack[slot, 1] = jnp.where(first_half, roll(zero, 64), one)
        copies[3].start()
        face_pack[slot, 2] = jnp.where(even, zero, roll(one, 32))
        copies[4].start()
        face_pack[slot, 3] = jnp.where(even, roll(zero, 96), one)
        copies[5].start()

    def wait_faces(slot):
        for copy in faces(slot):
            copy.wait_recv()

    def nodes(slot, devices, far_side):
        return [
            pltpu.make_async_remote_copy(
                src_ref=node_send.at[slot],
                dst_ref=node_recv.at[slot, far_side[side]],
                send_sem=node_out_sem.at[slot, side],
                recv_sem=node_in_sem.at[slot, far_side[side]],
                device_id=device,
                device_id_type=MESH,
            )
            for side, device in enumerate(devices)
        ]

    def middle_copies(slot):
        return nodes(slot, near, [1, 0, 3, 2, 5, 4])

    def coarse_copies(slot):
        return nodes(slot, coarse_near, [1, 0, 3, 2, 4])

    def pack(v):
        return pick(
            group16, [roll(v[16 * q : 16 * q + 16], 32 * q) for q in range(4)]
        )

    def unpack(v):
        return jnp.concatenate([roll(v, (128 - 32 * q) % 128) for q in range(4)], axis=0)

    def sib_copies():
        return [
            pltpu.make_async_remote_copy(
                src_ref=sib_send,
                dst_ref=sib_recv.at[i],
                send_sem=sib_out_sem.at[i],
                recv_sem=sib_in_sem.at[i],
                device_id=device,
                device_id_type=MESH,
            )
            for i, device in enumerate(siblings)
        ]

    def by_node(left, right):
        out = []
        for a in range(2):
            product = matmul(left[a], right[a])
            out.append(pick(group, [product[64 * g : 64 * g + 64] for g in range(4)]))
        return out

    def smooth(field):
        return by_node(smooth_l, [tall(field[0]), tall(field[1])])

    def inner(field):
        out = []
        for a in range(2):
            own = field[a]
            turned_y = roll(own, 64)
            turned_z = jnp.where(even, roll(own, 96), roll(own, 32))
            right = jnp.concatenate(
                [wide(own), wide(field[1 - a]), wide(turned_y), wide(turned_z)], axis=0
            )
            out.append(fold_fine(matmul(inner_l[a], right), group))
        return out

    def outer(slot):
        near_y, far_y = face_recv[slot, 2], face_recv[slot, 3]
        near_z, far_z = face_recv[slot, 4], face_recv[slot, 5]
        along_y = [
            jnp.where(first_half, near_y, roll(far_y, 64)),
            jnp.where(first_half, roll(near_y, 64), far_y),
        ]
        along_z = [
            jnp.where(even, near_z, roll(far_z, 32)),
            jnp.where(even, roll(near_z, 96), far_z),
        ]
        out = []
        for a in range(2):
            z = wide(along_z[a])
            right = jnp.concatenate([wide(face_recv[slot, a]), wide(along_y[a]), z, z], axis=0)
            out.append(fold_fine(matmul(outer_l[a], right), group))
        return out

    def one_smoothed(level, v):
        return matmul(one_smooth[level], tall(v))

    def one_apply(level, copies, slot, v):
        total = matmul(one_centre[level], tall(v))
        for copy in copies:
            copy.wait_recv()
        parts = [wide(unpack(node_recv[slot, side])) for side in range(len(copies))]
        if len(parts) == 5:
            parts.append(parts[4])
        product = matmul(one_outer[level], jnp.concatenate(parts, axis=0))
        return total + (
            (product[0:64, 0:128] + product[0:64, 128:256])
            + (product[64:128, 0:128] + product[64:128, 128:256])
        )

    def send_node(slot, copies, v):
        node_send[slot] = pack(v)
        for copy in copies:
            copy.start()

    def plus(x, y):
        return [p + q for p, q in zip(x, y)]

    def minus(x, y):
        return [p - q for p, q in zip(x, y)]

    def scaled(x, factor):
        return [p * factor for p in x]

    inverse, steps = coefficients(0)
    loads[1].wait()
    double_fine(fsmooth, smooth_l, 32)
    loads[0].wait()
    from_natural(rhs_raw, packed)
    resid = [packed[0], packed[1]]
    first = scaled(smooth(resid), inverse)
    pl.semaphore_wait(barrier, len(greeted))
    send_faces(0, first)

    loads[2].wait()
    prepare_fine()
    resid = minus(resid, inner(first))
    wait_faces(0)
    resid = minus(resid, outer(0))
    keep, push = steps[0]
    second = plus(scaled(first, keep), scaled(smooth(resid), push))
    send_faces(1, second)
    fine_first = plus(first, second)

    loads[3].wait()
    double_fine(fprolong, prolong_l, 40, restrict_l)
    loads[5].wait()
    one_block(msmooth, at["gz"], 4, one_smooth.at[0], 48)
    loads[4].wait()
    one_operator(
        mblocks, at["gz"], 4, lambda d: mlinks[0, 0, at["gz"], d - 1].astype(F32) * reach[d - 1], 0, 50
    )

    resid = minus(resid, inner(second))
    wait_faces(1)
    resid = minus(resid, outer(1))

    parts = []
    for a in range(2):
        for g in range(4):
            parts.append(wide(roll(resid[a], (128 - 32 * g) % 128)))
    product = matmul(restrict_l[...], jnp.concatenate(parts, axis=0))
    mid_resid = (product[0:64, 0:128] + product[0:64, 128:256]) + (
        product[64:128, 0:128] + product[64:128, 128:256]
    )
    mid_inverse, mid_steps = coefficients(1)
    mid_keep, mid_push = mid_steps[0]
    first = one_smoothed(0, mid_resid) * mid_inverse
    copies = middle_copies(0)
    send_node(0, copies, first)
    loads[6].wait()
    one_turned(one_block(mprolong, at["gz"], 4, one_prolong.at[0], 49), one_prolong.at[1])
    mid_resid = mid_resid - one_apply(0, copies, 0, first)
    second = first * mid_keep + one_smoothed(0, mid_resid) * mid_push
    copies = middle_copies(1)
    send_node(1, copies, second)
    mid_field = first + second
    loads[8].wait()
    one_block(csmooth, parent_z, 2, one_smooth.at[1], 54)
    loads[7].wait()
    one_operator(
        cblocks,
        parent_z,
        2,
        lambda d: clinks[0, d - 1, parent_z, parent_y].astype(F32) * coarse_reach[d - 1],
        1,
        55,
    )
    mid_resid = mid_resid - one_apply(0, copies, 1, second)

    own = pack(matmul(one_prolong[1], tall(mid_resid)))
    sib_send[...] = own
    copies = sib_copies()
    for copy in copies:
        copy.start()
    coarse_inverse, coarse_steps = coefficients(2)
    for copy in copies:
        copy.wait_recv()
    coarse_resid = unpack((own + sib_recv[0]) + (sib_recv[1] + sib_recv[2]))
    step = one_smoothed(1, coarse_resid) * coarse_inverse
    coarse_field = step
    for sweep in range(3):
        copies = coarse_copies(2 + sweep)
        send_node(2 + sweep, copies, step)
        coarse_resid = coarse_resid - one_apply(1, copies, 2 + sweep, step)
        keep, push = coarse_steps[sweep]
        step = step * keep + one_smoothed(1, coarse_resid) * push
        coarse_field = coarse_field + step

    lifted = matmul(one_prolong[0], tall(coarse_field))
    copies = middle_copies(5)
    send_node(5, copies, lifted)
    mid_field = mid_field + lifted
    mid_resid = mid_resid - one_apply(0, copies, 5, lifted)
    first = one_smoothed(0, mid_resid) * mid_inverse
    copies = middle_copies(6)
    send_node(6, copies, first)
    mid_field = mid_field + first
    mid_resid = mid_resid - one_apply(0, copies, 6, first)
    mid_field = mid_field + (first * mid_keep + one_smoothed(0, mid_resid) * mid_push)

    inverse, steps = coefficients(0)
    keep, push = steps[0]
    alone = jnp.where(group == 0, mid_field, 0.0)
    alone = alone + roll(alone, 32)
    alone = tall(alone + roll(alone, 64))
    lifted = by_node(prolong_l, [alone, alone])
    send_faces(2, lifted)
    fine_field = plus(fine_first, lifted)
    resid = minus(resid, inner(lifted))
    wait_faces(2)
    resid = minus(resid, outer(2))
    first = scaled(smooth(resid), inverse)
    send_faces(3, first)
    fine_field = plus(fine_field, first)
    resid = minus(resid, inner(first))
    wait_faces(3)
    resid = minus(resid, outer(3))
    second = plus(scaled(first, keep), scaled(smooth(resid), push))
    send_faces(4, second)
    fine_field = plus(fine_field, second)
    to_natural(fine_field, solution_ref)
    resid = minus(resid, inner(second))
    wait_faces(4)
    resid = minus(resid, outer(4))
    to_natural(resid, residual_ref)

    for slot in range(5):
        for copy in faces(slot):
            copy.wait_send()
    for slot in (0, 1, 5, 6):
        for copy in middle_copies(slot):
            copy.wait_send()
    for slot in (2, 3, 4):
        for copy in coarse_copies(slot):
            copy.wait_send()
    for copy in sib_copies():
        copy.wait_send()


def interleaved(x):
    nodes, n = x.shape[-2:]
    x = jnp.swapaxes(x.reshape(x.shape[:-1] + (n // 128, 128)), -3, -2)
    return x.reshape(x.shape[:-3] + (n // 128 * nodes, 128))


def by_link(x):
    return interleaved(jnp.swapaxes(x, -3, -2))


def body(*args):
    (rhs, fblocks, flinks, fsmooth, fprolong, mblocks, mlinks, msmooth, mprolong) = args[:9]
    (cblocks, clinks, csmooth, lowers, uppers) = args[9:]
    shape = rhs.shape
    rhs, fsmooth, fprolong = interleaved(rhs), interleaved(fsmooth), interleaved(fprolong)
    fblocks, mblocks, cblocks = by_link(fblocks), by_link(mblocks)[0, 0], by_link(cblocks)[0]
    msmooth, mprolong = interleaved(msmooth)[0, 0], interleaved(mprolong)[0, 0]
    csmooth = interleaved(csmooth)[0]
    clinks = jnp.transpose(clinks, (0, 3, 2, 1))
    anywhere = pl.BlockSpec(memory_space=pl.ANY)
    scalars = pl.BlockSpec(memory_space=pltpu.SMEM)
    vmem = pl.BlockSpec(memory_space=pltpu.VMEM)
    dma = pltpu.SemaphoreType.DMA
    outs = pl.pallas_call(
        kernel,
        out_shape=(
            jax.ShapeDtypeStruct(rhs.shape, F32),
            jax.ShapeDtypeStruct(rhs.shape, F32),
        ),
        in_specs=[
            anywhere,
            anywhere,
            scalars,
            anywhere,
            anywhere,
            anywhere,
            scalars,
            anywhere,
            anywhere,
            anywhere,
            scalars,
            anywhere,
            scalars,
            scalars,
        ],
        out_specs=(vmem, vmem),
        scratch_shapes=[
            pltpu.VMEM(rhs.shape, F32),
            pltpu.VMEM(fblocks.shape, F32),
            pltpu.VMEM(fsmooth.shape, F32),
            pltpu.VMEM(fprolong.shape, F32),
            pltpu.VMEM(mblocks.shape, F32),
            pltpu.VMEM(msmooth.shape, F32),
            pltpu.VMEM(mprolong.shape, F32),
            pltpu.VMEM(cblocks.shape[1:], F32),
            pltpu.VMEM(csmooth.shape[1:], F32),
            dma((9,)),
            pltpu.VMEM((2, 64, 128), F32),
            pltpu.VMEM((59, 64, 128), F32),
            pltpu.VMEM((2, 512, 256), BF16),
            pltpu.VMEM((2, 512, 256), BF16),
            pltpu.VMEM((2, 256, 256), BF16),
            pltpu.VMEM((2, 256, 256), BF16),
            pltpu.VMEM((128, 512), BF16),
            pltpu.VMEM((2, 128, 384), BF16),
            pltpu.VMEM((2, 64, 256), BF16),
            pltpu.VMEM((2, 64, 256), BF16),
            pltpu.VMEM((2, 64, 256), BF16),
            pltpu.VMEM((5, 2, 64, 128), F32),
            pltpu.VMEM((5, 4, 64, 128), F32),
            pltpu.VMEM((5, 6, 64, 128), F32),
            pltpu.VMEM((7, 16, 128), F32),
            pltpu.VMEM((7, 6, 16, 128), F32),
            pltpu.VMEM((16, 128), F32),
            pltpu.VMEM((3, 16, 128), F32),
            dma((5, 6)),
            dma((5, 6)),
            dma((7, 6)),
            dma((7, 6)),
            dma((3,)),
            dma((3,)),
        ],
        compiler_params=pltpu.CompilerParams(
            collective_id=0, has_side_effects=True, vmem_limit_bytes=56 * 1024 * 1024
        ),
    )(
        rhs,
        fblocks,
        flinks,
        fsmooth,
        fprolong,
        mblocks,
        mlinks,
        msmooth,
        mprolong,
        cblocks,
        clinks,
        csmooth,
        lowers,
        uppers,
    )
    return tuple(
        jnp.swapaxes(out.reshape(2, 2, 16, 2, 128), 2, 3).reshape(shape) for out in outs
    )


def solution(mesh):
    return jax.shard_map(
        body,
        mesh=mesh,
        in_specs=(
            P("gx", "gy", "gz", None),
            P("gx", "gy", "gz", None, None),
            P("gx", "gy", "gz", None),
            P("gx", "gy", "gz", None),
            P("gx", "gy", "gz", None),
            P("gx", "gy", None, None, None),
            P("gx", "gy", None, None),
            P("gx", "gy", None, None),
            P("gx", "gy", None, None),
            P("gx", None, None, None, None),
            P("gx", None, None, None),
            P("gx", None, None, None),
            P(),
            P(),
        ),
        out_specs=(P("gx", "gy", "gz", None), P("gx", "gy", "gz", None)),
        check_vma=False,
    )
```

```python
import jax
import jax.numpy as jnp
from jax import lax
from jax.experimental import pallas as pl
from jax.experimental.pallas import tpu as pltpu
from jax.sharding import PartitionSpec as P

F32 = jnp.float32
BF16 = jnp.bfloat16
MESH = pl.DeviceIdType.MESH


def lane(shape=(64, 128)):
    return lax.broadcasted_iota(jnp.int32, shape, 1)


def low(shape=(64, 128)):
    return lane(shape) < 64


def pick(group, parts):
    return jnp.where(
        group < 2,
        jnp.where(group == 0, parts[0], parts[1]),
        jnp.where(group == 2, parts[2], parts[3]),
    )


def roll(x, shift):
    return pltpu.roll(x, shift, 1) if shift else x


def split(v):
    high = v.astype(BF16)
    return high, (v - high.astype(F32)).astype(BF16)


def wide(v):
    return jnp.concatenate(split(v), axis=1)


def tall(v):
    high, rest = split(v)
    return jnp.concatenate([high, rest, high, rest], axis=0)


def matmul(left, right):
    return jnp.dot(left, right, preferred_element_type=F32)


def rows_of(ref, node, many):
    return ref[pl.ds(node, 32, stride=many), :]


def weave(ref, left, right):
    first = low((32, 128))
    left_turned, right_turned = roll(left, 64), roll(right, 64)
    ref[pl.ds(0, 32, stride=2), :] = jnp.where(first, left, right_turned)
    ref[pl.ds(1, 32, stride=2), :] = jnp.where(first, left_turned, right)
    return ref[...]


def double(block):
    high, rest = split(block)
    return jnp.concatenate([high, rest], axis=1)


def fold_fine(product, group):
    total = (product[:256, :128] + product[:256, 128:]) + (
        product[256:, :128] + product[256:, 128:]
    )
    return pick(group, [total[64 * g : 64 * g + 64] for g in range(4)])


def kernel(
    rhs_hbm,
    fblocks_hbm,
    flinks_hbm,
    fsmooth_hbm,
    fprolong_hbm,
    mblocks_hbm,
    mlinks_hbm,
    msmooth_hbm,
    mprolong_hbm,
    cblocks_hbm,
    clinks_hbm,
    csmooth_hbm,
    lowers_hbm,
    uppers_hbm,
    solution_ref,
    residual_ref,
    flinks,
    mlinks,
    clinks,
    lowers,
    uppers,
    rhs_raw,
    fblocks,
    fsmooth,
    fprolong,
    mblocks,
    msmooth,
    mprolong,
    cblocks,
    csmooth,
    in_sems,
    packed,
    woven,
    inner_l,
    outer_l,
    smooth_l,
    prolong_l,
    restrict_l,
    one_outer,
    one_centre,
    one_smooth,
    one_prolong,
    face_send,
    face_pack,
    face_recv,
    node_send,
    node_recv,
    term_send,
    term_recv,
    block_send,
    block_recv,
    near_smooth,
    face_out_sem,
    face_in_sem,
    node_out_sem,
    node_in_sem,
    term_out_sem,
    term_in_sem,
    block_out_sem,
    block_in_sem,
):
    size = {name: lax.axis_size(name) for name in ("gx", "gy", "gz")}
    at = {name: lax.axis_index(name) for name in ("gx", "gy", "gz")}

    def beside(name, step):
        return {name: lax.rem(at[name] + (step + size[name]), size[name])}

    mate_y = at["gy"] + 1 - 2 * lax.rem(at["gy"], 2)
    mate_z = at["gz"] + 1 - 2 * lax.rem(at["gz"], 2)
    near = [
        beside("gx", -1),
        beside("gx", 1),
        beside("gy", -1),
        beside("gy", 1),
        beside("gz", -1),
        beside("gz", 1),
    ]
    coarse_near = [
        beside("gx", -1),
        beside("gx", 1),
        beside("gy", -2),
        beside("gy", 2),
        beside("gz", 2),
    ]

    def four(shift):
        name, step = shift
        place = dict(at)
        mates = {"gy": mate_y, "gz": mate_z}
        if name is not None:
            place[name] = lax.rem(at[name] + (step + size[name]), size[name])
        if name in mates:
            mates[name] = lax.rem(mates[name] + (step + size[name]), size[name])
        return [
            place,
            {**place, "gy": mates["gy"]},
            {**place, "gz": mates["gz"]},
            {**place, **mates},
        ]

    shifts = [(None, 0), ("gx", -1), ("gx", 1), ("gy", -2), ("gy", 2), ("gz", 2)]
    across = [0, 2, 1, 4, 3, 5]
    holders = [(m, e, device) for m in range(6) for e, device in enumerate(four(shifts[m]))][1:]
    parent_y = lax.div(at["gy"], 2)
    parent_z = lax.div(at["gz"], 2)

    barrier = pltpu.get_barrier_semaphore()
    for _, _, device in holders:
        pl.semaphore_signal(barrier, inc=1, device_id=device, device_id_type=MESH)

    loads = [
        pltpu.make_async_copy(src, dst, in_sems.at[i])
        for i, (src, dst) in enumerate(
            [
                (fsmooth_hbm, fsmooth),
                (rhs_hbm, rhs_raw),
                (lowers_hbm, lowers),
                (uppers_hbm, uppers),
                (flinks_hbm, flinks),
                (fblocks_hbm, fblocks),
                (fprolong_hbm, fprolong),
                (msmooth_hbm, msmooth),
                (mlinks_hbm, mlinks),
                (mblocks_hbm, mblocks),
                (mprolong_hbm, mprolong),
                (csmooth_hbm, csmooth),
                (clinks_hbm, clinks),
                (cblocks_hbm.at[parent_y], cblocks),
            ]
        )
    ]
    for load in loads:
        load.start()

    def has(name, step):
        if step < 0:
            return jnp.where(at[name] >= -step, 1.0, 0.0).astype(F32)
        return jnp.where(at[name] < size[name] - step, 1.0, 0.0).astype(F32)

    reach = [has("gx", -1), has("gx", 1), has("gy", -1), has("gy", 1), has("gz", -1), has("gz", 1)]
    coarse_reach = [has("gx", -1), has("gx", 1), has("gy", -2), has("gy", 2), has("gz", -2), has("gz", 2)]

    group = lax.shift_right_logical(lane(), 5)
    group16 = lax.shift_right_logical(lane((16, 128)), 5)
    first_half = low()
    even = lax.rem(group, 2) == 0

    def coefficients(level):
        upper = jnp.full((1, 128), uppers[level], F32)
        lower = jnp.full((1, 128), lowers[level], F32)
        theta = (upper + lower) * 0.5
        delta = (upper - lower) * 0.5
        sigma = theta / delta
        rho = 1.0 / sigma
        steps = []
        for _ in range(3 if level == 2 else 1):
            later = 1.0 / (2.0 * sigma - rho)
            steps.append((later * rho, 2.0 * later / delta))
            rho = later
        return 1.0 / theta, steps

    def from_natural(raw, out):
        for a in range(2):
            nodes = [raw[a, g // 2, pl.ds(g % 2, 16, stride=2), :] for g in range(4)]
            for q in range(4):
                out[a, pl.ds(q, 16, stride=4), :] = pick(
                    group16, [roll(nodes[g], 32 * ((g - q) % 4)) for g in range(4)]
                )

    def to_natural(field, out):
        for a in range(2):
            packed[a] = field[a]
        for a in range(2):
            rows = [packed[a, pl.ds(q, 16, stride=4), :] for q in range(4)]
            for g in range(4):
                out[a, g // 2, pl.ds(g % 2, 16, stride=2), :] = pick(
                    group16, [roll(rows[q], 32 * ((q - g) % 4)) for q in range(4)]
                )

    def each(times, body):
        def step(n, carry):
            body(n)
            return carry

        lax.fori_loop(0, times, step, 0)

    def put(ref, a, g, column, value, rest_at=256):
        high, rest = split(value)
        rows = pl.ds(pl.multiple_of(g * 64, 64), 64)
        rest_rows = pl.ds(pl.multiple_of(rest_at + g * 64, 64), 64)
        ref[a, rows, column : column + 128] = high
        ref[a, rest_rows, column : column + 128] = rest

    def double_fine(raw, out, slot, turned=None):
        for a in range(2):
            for b in range(2):
                both = []
                for c in range(2):
                    g = 2 * b + c
                    block = rows_of(raw.at[a, b], c, 2)
                    block = weave(woven.at[slot + 4 * a + g], block, block)
                    out[a, 64 * g : 64 * g + 64, :] = double(block)
                    both.append(block)
                if turned is not None:
                    column = 128 * (2 * a + b)
                    high, rest = split(jnp.transpose(jnp.concatenate(both, axis=0))[0:64, :])
                    turned[0:64, column : column + 128] = high
                    turned[64:128, column : column + 128] = rest

    def prepare_fine():
        def body(n):
            a, b = lax.div(n, 2), lax.rem(n, 2)

            def far(axis, here):
                return jnp.where(here == 0, reach[2 * axis], reach[2 * axis + 1])

            for c in range(2):
                g = 2 * b + c

                def block(d, far=None):
                    flag = flinks[a, b, c, d - 1].astype(F32)
                    if far is not None:
                        flag = flag * far
                    return rows_of(fblocks.at[a, b, d], c, 2) * flag

                slots = woven.at[pl.ds(n * 8 + c * 4, 4)]
                centre = rows_of(fblocks.at[a, b, 0], c, 2)
                put(inner_l, a, g, 0, weave(slots.at[0], centre, block(2 - a)))
                put(inner_l, a, g, 128, weave(slots.at[1], block(4 - b), block(6 - c)))
                put(outer_l, a, g, 0, weave(slots.at[2], block(1 + a, far(0, a)), block(3 + b, far(1, b))))
                last = block(5 + c, far(2, c))
                put(outer_l, a, g, 128, weave(slots.at[3], last, jnp.zeros_like(last)))

        each(4, body)

    def one_block(raw, row, many, out, slot):
        block = rows_of(raw, row, many)
        block = weave(woven.at[slot], block, block)
        out[...] = double(block)
        return block

    def one_turned(block, out):
        out[...] = double(jnp.transpose(jnp.concatenate([block, block], axis=0))[0:64, :])

    def one_operator(raw, row, many, flag, level, slot):
        one_block(raw.at[0], row, many, one_centre.at[level], slot)
        for pair in range(3):
            d = 2 * pair + 1
            put(
                one_outer,
                level,
                0,
                128 * pair,
                weave(
                    woven.at[slot + 1 + pair],
                    rows_of(raw.at[d], row, many) * flag(d),
                    rows_of(raw.at[d + 1], row, many) * flag(d + 1),
                ),
                64,
            )

    def faces(slot):
        copies = []
        for side in range(6):
            if side == 0:
                src, dst = face_send.at[slot, 0], 1
            elif side == 1:
                src, dst = face_send.at[slot, 1], 0
            else:
                src, dst = face_pack.at[slot, side - 2], side ^ 1
            copies.append(
                pltpu.make_async_remote_copy(
                    src_ref=src,
                    dst_ref=face_recv.at[slot, dst],
                    send_sem=face_out_sem.at[slot, side],
                    recv_sem=face_in_sem.at[slot, dst],
                    device_id=near[side],
                    device_id_type=MESH,
                )
            )
        return copies

    def send_faces(slot, field):
        copies = faces(slot)
        zero, one = field
        face_send[slot, 0] = zero
        face_send[slot, 1] = one
        copies[0].start()
        copies[1].start()
        face_pack[slot, 0] = jnp.where(first_half, zero, roll(one, 64))
        copies[2].start()
        face_pack[slot, 1] = jnp.where(first_half, roll(zero, 64), one)
        copies[3].start()
        face_pack[slot, 2] = jnp.where(even, zero, roll(one, 32))
        copies[4].start()
        face_pack[slot, 3] = jnp.where(even, roll(zero, 96), one)
        copies[5].start()

    def wait_faces(slot):
        for copy in faces(slot):
            copy.wait_recv()

    def nodes(slot, devices, far_side):
        return [
            pltpu.make_async_remote_copy(
                src_ref=node_send.at[slot],
                dst_ref=node_recv.at[slot, far_side[side]],
                send_sem=node_out_sem.at[slot, side],
                recv_sem=node_in_sem.at[slot, far_side[side]],
                device_id=device,
                device_id_type=MESH,
            )
            for side, device in enumerate(devices)
        ]

    def middle_copies(slot):
        return nodes(slot, near, [1, 0, 3, 2, 5, 4])

    def coarse_copies(slot):
        return nodes(slot, coarse_near, [1, 0, 3, 2, 4])

    def pack(v):
        return pick(
            group16, [roll(v[16 * q : 16 * q + 16], 32 * q) for q in range(4)]
        )

    def unpack(v):
        return jnp.concatenate([roll(v, (128 - 32 * q) % 128) for q in range(4)], axis=0)

    def term_copies():
        return [
            pltpu.make_async_remote_copy(
                src_ref=term_send,
                dst_ref=term_recv.at[4 * across[m] + e],
                send_sem=term_out_sem.at[4 * m + e],
                recv_sem=term_in_sem.at[4 * across[m] + e],
                device_id=device,
                device_id_type=MESH,
            )
            for m, e, device in holders
        ]

    def block_copies():
        return [
            pltpu.make_async_remote_copy(
                src_ref=block_send,
                dst_ref=block_recv.at[1 - side],
                send_sem=block_out_sem.at[side],
                recv_sem=block_in_sem.at[1 - side],
                device_id=near[side],
                device_id_type=MESH,
            )
            for side in range(2)
        ]

    def by_node(left, right):
        out = []
        for a in range(2):
            product = matmul(left[a], right[a])
            out.append(pick(group, [product[64 * g : 64 * g + 64] for g in range(4)]))
        return out

    def smooth(field):
        return by_node(smooth_l, [tall(field[0]), tall(field[1])])

    def inner(field):
        out = []
        for a in range(2):
            own = field[a]
            turned_y = roll(own, 64)
            turned_z = jnp.where(even, roll(own, 96), roll(own, 32))
            right = jnp.concatenate(
                [wide(own), wide(field[1 - a]), wide(turned_y), wide(turned_z)], axis=0
            )
            out.append(fold_fine(matmul(inner_l[a], right), group))
        return out

    def outer(slot):
        near_y, far_y = face_recv[slot, 2], face_recv[slot, 3]
        near_z, far_z = face_recv[slot, 4], face_recv[slot, 5]
        along_y = [
            jnp.where(first_half, near_y, roll(far_y, 64)),
            jnp.where(first_half, roll(near_y, 64), far_y),
        ]
        along_z = [
            jnp.where(even, near_z, roll(far_z, 32)),
            jnp.where(even, roll(near_z, 96), far_z),
        ]
        out = []
        for a in range(2):
            z = wide(along_z[a])
            right = jnp.concatenate([wide(face_recv[slot, a]), wide(along_y[a]), z, z], axis=0)
            out.append(fold_fine(matmul(outer_l[a], right), group))
        return out

    def one_smoothed(level, v):
        return matmul(one_smooth[level], tall(v))

    def one_outside(level, parts):
        if len(parts) == 5:
            parts = parts + [parts[4]]
        product = matmul(one_outer[level], jnp.concatenate(parts, axis=0))
        return (product[0:64, 0:128] + product[0:64, 128:256]) + (
            product[64:128, 0:128] + product[64:128, 128:256]
        )

    def one_apply(level, copies, slot, v):
        total = matmul(one_centre[level], tall(v))
        for copy in copies:
            copy.wait_recv()
        parts = [wide(unpack(node_recv[slot, side])) for side in range(len(copies))]
        return total + one_outside(level, parts)

    def send_node(slot, copies, v):
        node_send[slot] = pack(v)
        for copy in copies:
            copy.start()

    def plus(x, y):
        return [p + q for p, q in zip(x, y)]

    def minus(x, y):
        return [p - q for p, q in zip(x, y)]

    def scaled(x, factor):
        return [p * factor for p in x]

    loads[0].wait()
    double_fine(fsmooth, smooth_l, 32)
    loads[1].wait()
    from_natural(rhs_raw, packed)
    loads[2].wait()
    loads[3].wait()
    inverse, steps = coefficients(0)
    resid = [packed[0], packed[1]]
    first = scaled(smooth(resid), inverse)
    pl.semaphore_wait(barrier, len(holders))
    send_faces(0, first)

    loads[4].wait()
    loads[5].wait()
    prepare_fine()
    loads[11].wait()
    block_send[...] = rows_of(csmooth.at[parent_y], parent_z, 2)
    for copy in block_copies():
        copy.start()
    resid = minus(resid, inner(first))
    wait_faces(0)
    resid = minus(resid, outer(0))
    keep, push = steps[0]
    second = plus(scaled(first, keep), scaled(smooth(resid), push))
    send_faces(1, second)
    fine_first = plus(first, second)

    loads[6].wait()
    double_fine(fprolong, prolong_l, 40, restrict_l)
    loads[7].wait()
    one_block(msmooth, at["gz"], 4, one_smooth.at[0], 48)
    loads[8].wait()
    loads[9].wait()
    one_operator(
        mblocks, at["gz"], 4, lambda d: mlinks[0, 0, at["gz"], d - 1].astype(F32) * reach[d - 1], 0, 50
    )

    resid = minus(resid, inner(second))
    wait_faces(1)
    resid = minus(resid, outer(1))

    parts = []
    for a in range(2):
        for g in range(4):
            parts.append(wide(roll(resid[a], (128 - 32 * g) % 128)))
    product = matmul(restrict_l[...], jnp.concatenate(parts, axis=0))
    mid_resid = (product[0:64, 0:128] + product[0:64, 128:256]) + (
        product[64:128, 0:128] + product[64:128, 128:256]
    )
    mid_inverse, mid_steps = coefficients(1)
    mid_keep, mid_push = mid_steps[0]
    first = one_smoothed(0, mid_resid) * mid_inverse
    copies = middle_copies(0)
    send_node(0, copies, first)
    loads[10].wait()
    one_turned(one_block(mprolong, at["gz"], 4, one_prolong.at[0], 49), one_prolong.at[1])
    mid_resid = mid_resid - one_apply(0, copies, 0, first)
    second = first * mid_keep + one_smoothed(0, mid_resid) * mid_push
    copies = middle_copies(1)
    send_node(1, copies, second)
    mid_field = first + second
    one_block(csmooth.at[parent_y], parent_z, 2, one_smooth.at[1], 54)
    levels_y = lax.div(size["gy"], 2)
    beside_y = [lax.rem(parent_y + (levels_y + step), levels_y) for step in (-1, 1)]
    one_block(csmooth.at[beside_y[0]], parent_z, 2, near_smooth.at[2], 61)
    one_block(csmooth.at[beside_y[1]], parent_z, 2, near_smooth.at[3], 62)
    one_block(csmooth.at[parent_y], 1 - parent_z, 2, near_smooth.at[4], 63)
    for side, copy in enumerate(block_copies()):
        copy.wait_recv()
    for side in range(2):
        block = block_recv[side]
        near_smooth[side] = double(weave(woven.at[59 + side], block, block))
    loads[12].wait()
    loads[13].wait()
    one_operator(
        cblocks,
        parent_z,
        2,
        lambda d: clinks[0, d - 1, parent_z, parent_y].astype(F32) * coarse_reach[d - 1],
        1,
        55,
    )
    mid_resid = mid_resid - one_apply(0, copies, 1, second)

    own = pack(matmul(one_prolong[1], tall(mid_resid)))
    term_send[...] = own
    terms = term_copies()
    for copy in terms:
        copy.start()
    coarse_inverse, coarse_steps = coefficients(2)
    for copy in terms:
        copy.wait_recv()

    def total(m):
        first = own if m == 0 else term_recv[4 * m]
        return unpack(
            (first + term_recv[4 * m + 1]) + (term_recv[4 * m + 2] + term_recv[4 * m + 3])
        )

    coarse_resid = total(0)
    step = one_smoothed(1, coarse_resid) * coarse_inverse
    parts = [
        wide(matmul(near_smooth[m - 1], tall(total(m))) * coarse_inverse) for m in range(1, 6)
    ]
    coarse_field = step
    for sweep in range(3):
        if sweep == 0:
            change = matmul(one_centre[1], tall(step)) + one_outside(1, parts)
        else:
            copies = coarse_copies(2 + sweep)
            send_node(2 + sweep, copies, step)
            change = one_apply(1, copies, 2 + sweep, step)
        coarse_resid = coarse_resid - change
        keep, push = coarse_steps[sweep]
        step = step * keep + one_smoothed(1, coarse_resid) * push
        coarse_field = coarse_field + step

    lifted = matmul(one_prolong[0], tall(coarse_field))
    copies = middle_copies(5)
    send_node(5, copies, lifted)
    mid_field = mid_field + lifted
    mid_resid = mid_resid - one_apply(0, copies, 5, lifted)
    first = one_smoothed(0, mid_resid) * mid_inverse
    copies = middle_copies(6)
    send_node(6, copies, first)
    mid_field = mid_field + first
    mid_resid = mid_resid - one_apply(0, copies, 6, first)
    mid_field = mid_field + (first * mid_keep + one_smoothed(0, mid_resid) * mid_push)

    inverse, steps = coefficients(0)
    keep, push = steps[0]
    alone = jnp.where(group == 0, mid_field, 0.0)
    alone = alone + roll(alone, 32)
    alone = tall(alone + roll(alone, 64))
    lifted = by_node(prolong_l, [alone, alone])
    send_faces(2, lifted)
    fine_field = plus(fine_first, lifted)
    resid = minus(resid, inner(lifted))
    wait_faces(2)
    resid = minus(resid, outer(2))
    first = scaled(smooth(resid), inverse)
    send_faces(3, first)
    fine_field = plus(fine_field, first)
    resid = minus(resid, inner(first))
    wait_faces(3)
    resid = minus(resid, outer(3))
    second = plus(scaled(first, keep), scaled(smooth(resid), push))
    send_faces(4, second)
    fine_field = plus(fine_field, second)
    to_natural(fine_field, solution_ref)
    resid = minus(resid, inner(second))
    wait_faces(4)
    resid = minus(resid, outer(4))
    to_natural(resid, residual_ref)

    for slot in range(5):
        for copy in faces(slot):
            copy.wait_send()
    for slot in (0, 1, 5, 6):
        for copy in middle_copies(slot):
            copy.wait_send()
    for slot in (3, 4):
        for copy in coarse_copies(slot):
            copy.wait_send()
    for copy in term_copies() + block_copies():
        copy.wait_send()


def interleaved(x):
    nodes, n = x.shape[-2:]
    x = jnp.swapaxes(x.reshape(x.shape[:-1] + (n // 128, 128)), -3, -2)
    return x.reshape(x.shape[:-3] + (n // 128 * nodes, 128))


def by_link(x):
    return interleaved(jnp.swapaxes(x, -3, -2))


def body(*args):
    (rhs, fblocks, flinks, fsmooth, fprolong, mblocks, mlinks, msmooth, mprolong) = args[:9]
    (cblocks, clinks, csmooth, lowers, uppers) = args[9:]
    shape = rhs.shape
    rhs, fsmooth, fprolong = interleaved(rhs), interleaved(fsmooth), interleaved(fprolong)
    fblocks, mblocks, cblocks = by_link(fblocks), by_link(mblocks)[0, 0], by_link(cblocks)[0]
    msmooth, mprolong = interleaved(msmooth)[0, 0], interleaved(mprolong)[0, 0]
    csmooth = interleaved(csmooth)[0]
    clinks = jnp.transpose(clinks, (0, 3, 2, 1))
    anywhere = pl.BlockSpec(memory_space=pl.ANY)
    dma = pltpu.SemaphoreType.DMA
    outs = pl.pallas_call(
        kernel,
        out_shape=(pltpu.VMEM(rhs.shape, F32), pltpu.VMEM(rhs.shape, F32)),
        in_specs=[anywhere] * 14,
        out_specs=(pl.BlockSpec(memory_space=pltpu.VMEM),) * 2,
        scratch_shapes=[
            pltpu.SMEM(flinks.shape, jnp.int32),
            pltpu.SMEM(mlinks.shape, jnp.int32),
            pltpu.SMEM(clinks.shape, jnp.int32),
            pltpu.SMEM(lowers.shape, F32),
            pltpu.SMEM(uppers.shape, F32),
            pltpu.VMEM(rhs.shape, F32),
            pltpu.VMEM(fblocks.shape, F32),
            pltpu.VMEM(fsmooth.shape, F32),
            pltpu.VMEM(fprolong.shape, F32),
            pltpu.VMEM(mblocks.shape, F32),
            pltpu.VMEM(msmooth.shape, F32),
            pltpu.VMEM(mprolong.shape, F32),
            pltpu.VMEM(cblocks.shape[1:], F32),
            pltpu.VMEM(csmooth.shape, F32),
            dma((14,)),
            pltpu.VMEM((2, 64, 128), F32),
            pltpu.VMEM((64, 64, 128), F32),
            pltpu.VMEM((2, 512, 256), BF16),
            pltpu.VMEM((2, 512, 256), BF16),
            pltpu.VMEM((2, 256, 256), BF16),
            pltpu.VMEM((2, 256, 256), BF16),
            pltpu.VMEM((128, 512), BF16),
            pltpu.VMEM((2, 128, 384), BF16),
            pltpu.VMEM((2, 64, 256), BF16),
            pltpu.VMEM((2, 64, 256), BF16),
            pltpu.VMEM((2, 64, 256), BF16),
            pltpu.VMEM((5, 2, 64, 128), F32),
            pltpu.VMEM((5, 4, 64, 128), F32),
            pltpu.VMEM((5, 6, 64, 128), F32),
            pltpu.VMEM((7, 16, 128), F32),
            pltpu.VMEM((7, 6, 16, 128), F32),
            pltpu.VMEM((16, 128), F32),
            pltpu.VMEM((24, 16, 128), F32),
            pltpu.VMEM((32, 128), F32),
            pltpu.VMEM((2, 32, 128), F32),
            pltpu.VMEM((5, 64, 256), BF16),
            dma((5, 6)),
            dma((5, 6)),
            dma((7, 6)),
            dma((7, 6)),
            dma((24,)),
            dma((24,)),
            dma((2,)),
            dma((2,)),
        ],
        compiler_params=pltpu.CompilerParams(
            collective_id=0, has_side_effects=True, vmem_limit_bytes=56 * 1024 * 1024
        ),
    )(
        rhs,
        fblocks,
        flinks,
        fsmooth,
        fprolong,
        mblocks,
        mlinks,
        msmooth,
        mprolong,
        cblocks,
        clinks,
        csmooth,
        lowers,
        uppers,
    )
    return tuple(
        jnp.swapaxes(out.reshape(2, 2, 16, 2, 128), 2, 3).reshape(shape) for out in outs
    )


def solution(mesh):
    return jax.shard_map(
        body,
        mesh=mesh,
        in_specs=(
            P("gx", "gy", "gz", None),
            P("gx", "gy", "gz", None, None),
            P("gx", "gy", "gz", None),
            P("gx", "gy", "gz", None),
            P("gx", "gy", "gz", None),
            P("gx", "gy", None, None, None),
            P("gx", "gy", None, None),
            P("gx", "gy", None, None),
            P("gx", "gy", None, None),
            P("gx", None, None, None, None),
            P("gx", None, None, None),
            P("gx", None, None, None),
            P(),
            P(),
        ),
        out_specs=(P("gx", "gy", "gz", None), P("gx", "gy", "gz", None)),
        check_vma=False,
    )
```
